32 devices in a mesh: groups: 2 (over y), dev: 8 (over z, x), sub: 2 (over core).
Axes of the slice: x: 2, y: 2, z: 4, core: 2. Of those that a mesh axis runs over, the one named last changes fastest.
Arguments:
- hidden: bfloat16 [2, 512, 3584], P(None, ('groups', 'dev')), parts along dimension 1, may hold values from -6 to 6
- norm_gain: float32 [3584], replicated, may hold values from 0.1 to 1.9
- routes: int32 [2, 512, 2], P(None, ('groups', 'dev')), parts along dimension 1, may hold values from 0 to 3, all different within a row; in each aligned block of 32 rows (0 to 31, 32 to 63, ..., all dimensions but the last counted through in order) at most 32 rows name the same one
- route_weight: float32 [2, 512, 2], P(None, ('groups', 'dev')), parts along dimension 1, may hold values from 0.1 to 1
- w_in: bfloat16 [3584, 4096], P(None, ('dev', 'sub')), may hold values from -0.09375 to 0.09375
- w_out: bfloat16 [4096, 3584], P(('dev', 'sub')), may hold values from -0.1875 to 0.1875
Outputs:
- layer_out: bfloat16 [2, 512, 3584], P(None, ('groups', 'dev'), 'sub'), parts along dimension 1
The draws below stay inside these ranges and needn't reach their ends.
There are 2 independent parts, one for each index of `groups`. The reference program is written for one: setup_inputs(seed, part) draws one part's arguments, and reference() takes and returns one part's arrays. A program takes and returns all parts, laid end to end along the dimension named above; an argument that names none is the same for every part. Nothing has to cross between parts.
Inputs may be any that keep to these rules, and one draw needn't show every extreme that they name: `routes`: each row names 2 different experts; in each micro-batch the 32 rows of one index of dev name one expert at most 32 times.
All inputs are finite; a program needn't handle non-finite values.
Results may differ from the reference program's by a relative error of at most 0.008.
Values may be sent and summed in bfloat16 or wider, within the bound.
No kernel may reach another device: no remote copies, remote signals or barrier semaphores. Data moves between devices by JAX's collectives and lax.ppermute only.
A program may use at most 64 MiB of HBM per device.

```python
import math
import jax
import jax.numpy as jnp
import numpy as np
from jax import lax

D = 3584
FE = 1024
TOP = 2
MB = 2
R = 32
EXPERTS = 4
CAP = 32
ROWS = 256
N_DEV = 8
N_SUB = 2


def steps_of(stream_key, extent, shards, smallest, high):
    def one(dim, blocks):
        draws = jax.random.uniform(jax.random.fold_in(jax.random.fold_in(stream_key, 6), dim), (blocks,), jnp.float32, smallest / len(shards), high / len(shards))
        return jnp.repeat(jnp.exp(draws), extent[dim] // blocks).reshape((-1,) + (1,) * (len(extent) - dim - 1))

    factor_of = one(*shards[0])
    for cut in shards[1:]:
        factor_of = factor_of * one(*cut)
    return factor_of


def assign_block(own_key, own, number, rows, count, top, limit, lean):
    sequence = jax.random.permutation(own_key, count)
    packed, common = shares(count, rows * top, limit, lean, True), shares(count, rows * top, limit, lean, False)
    places = jnp.arange(count)

    def named(sizes, offset_by):
        used = int((sizes > 0).sum())
        fixed = max(1, used // 4)
        passed = fixed + (places - fixed + offset_by * (used - fixed)) % max(1, count - fixed)
        return jnp.zeros((count,), jnp.int32).at[sequence[jnp.where(places < fixed, places, passed)]].set(jnp.asarray(sizes, jnp.int32))

    sizes = jnp.where(number % 4 == 0, named(packed, number // 4), named(common, number - number // 4 - 1))
    mixed = jax.random.permutation(jax.random.fold_in(own, 3), count)
    giver, receiver = mixed[0:count // 2 * 2:2], mixed[1:count // 2 * 2:2]
    slack = jnp.minimum(sizes[giver] - 1, limit - sizes[receiver]) // 2
    slack = jnp.where((giver == sequence[0]) | (receiver == sequence[0]) | (sizes[receiver] == 0), 0, jnp.maximum(slack, 0))
    passed = jax.random.randint(jax.random.fold_in(own, 4), (count // 2,), 0, 1 << 20) % (slack + 1)
    sizes = sizes.at[giver].add(-passed).at[receiver].add(passed)
    members = jnp.searchsorted(jnp.cumsum(sizes), jnp.arange(rows * top), side="right").astype(jnp.int32)
    grid = members.reshape(top, rows).T
    grid = grid[jax.random.permutation(jax.random.fold_in(own, 1), rows)]
    offset_by = jax.random.randint(jax.random.fold_in(own, 2), (rows, 1), 0, top)
    return jnp.take_along_axis(grid, (jnp.arange(top)[None, :] + offset_by) % top, axis=1)


def shares(amount, total, bound, skew, full):
    weights = [(1 << 20) // math.isqrt(grade ** skew) + 1 for grade in range(1, amount + 1)]
    largest = bound if full else min(bound, max(-(-total // amount), total * weights[0] // sum(weights)))
    least = 1 if total - largest >= amount - 1 else 0
    given, surplus = [largest] + [least] * (amount - 1), total - largest - least * (amount - 1)
    while surplus > 0:
        free = [i for i in range(1, amount) if given[i] < largest] or [i for i in range(1, amount) if given[i] < bound]
        whole, budget = sum([weights[i] for i in free]), surplus
        for i in free:
            more = min(bound - given[i], max(1, budget * weights[i] // whole), surplus)
            given[i] = given[i] + more
            surplus = surplus - more
    return np.array(given)


def gaussian(key, shape, spread, bound, split=(), held_as=jnp.bfloat16):
    array = jax.random.normal(key, shape, jnp.float32) * spread
    if len(split) > 0:
        array = steps_of(key, shape, split, -0.22, 0.18) * array
    return jnp.clip(array, min=-bound, max=bound).astype(held_as)


def setup_inputs(seed: int = 0, part: int = 0) -> dict:
    keys = jax.random.split(jax.random.key(seed), 7)
    own_keys = jax.random.split(jax.random.fold_in(keys[6], part), 7)
    hidden = gaussian(own_keys[0], (MB, ROWS, D), 1.0, 6.0, ((1, 8),))
    norm_gain = jnp.clip(1.0 + 0.18 * jax.random.normal(keys[1], (D,), jnp.float32), 0.1, 1.9)
    routes_keys = jax.random.split(jax.random.fold_in(own_keys[2], 1), MB * ROWS // R)
    routes_turns = jax.random.permutation(jax.random.fold_in(own_keys[2], 3), MB * ROWS // R)
    routes = jax.vmap(lambda own, number: assign_block(jax.random.fold_in(own_keys[2], 2), own, number, R, EXPERTS, TOP, CAP, 2))(routes_keys, routes_turns).reshape((MB, ROWS, TOP))
    route_weight = jnp.clip(0.1 + 0.9 * jax.random.uniform(own_keys[3], (MB, ROWS, TOP), jnp.float32) ** steps_of(own_keys[3], (MB, ROWS, TOP), ((1, 8),), -0.2, 0.2), 0.1, 1.0)
    w_in = gaussian(keys[4], (D, EXPERTS * FE), D ** -0.5, 0.09375, ((1, 16),))
    w_out = gaussian(keys[5], (EXPERTS * FE, D), FE ** -0.5, 0.1875, ((0, 16),))
    return dict(hidden=hidden, norm_gain=norm_gain, routes=routes, route_weight=route_weight, w_in=w_in, w_out=w_out)


EPS = 1e-06

def expert_block(hidden, norm_gain, routes, route_weight, w_in, w_out):
    highest = lax.Precision.HIGHEST
    hid = hidden.astype(jnp.float32)
    normed = (hid * lax.rsqrt(lax.optimization_barrier(jnp.mean(hid * hid, axis=-1, keepdims=True)) + EPS) * norm_gain.astype(jnp.float32)).astype(jnp.bfloat16)
    rows_all = MB * ROWS
    flat_rows = jnp.concatenate([normed.reshape(rows_all, D), jnp.zeros((1, D), jnp.bfloat16)], axis=0)
    slots = routes.reshape(-1).astype(jnp.int32)
    pairs = slots.shape[0]
    pair_row = jnp.concatenate([jnp.repeat(jnp.arange(rows_all, dtype=jnp.int32), TOP), jnp.full((1,), rows_all, jnp.int32)])
    pair_weight = jnp.concatenate([route_weight.reshape(-1).astype(jnp.float32), jnp.zeros((1,), jnp.float32)])
    pieces = 2 * N_SUB
    piece_width = FE // pieces
    group_cap = MB * N_DEV * CAP

    def one_group(slot):
        take = jnp.nonzero(slots == slot, size=group_cap, fill_value=pairs)[0].astype(jnp.int32)
        rows = pair_row[take]
        weights = pair_weight[take]
        inputs = flat_rows[rows]
        start = (slot * FE).astype(jnp.int32)
        w_in_g = lax.dynamic_slice_in_dim(w_in, start, FE, 1)
        w_out_g = lax.dynamic_slice_in_dim(w_out, start, FE, 0)
        inner = jnp.dot(inputs, w_in_g, preferred_element_type=jnp.float32)
        act = jax.nn.silu(inner).astype(jnp.bfloat16)
        piece_out = jnp.einsum('nsu,sud->nsd', act.reshape(group_cap, pieces, piece_width).astype(jnp.float32), w_out_g.reshape(pieces, piece_width, D).astype(jnp.float32), precision=highest).astype(jnp.bfloat16)
        contrib = lax.optimization_barrier(jnp.sum(piece_out.astype(jnp.float32), axis=1)) * weights[:, None]
        return (rows, contrib)
    rows, contrib = lax.map(one_group, jnp.arange(EXPERTS, dtype=jnp.int32))
    total = jnp.zeros((rows_all + 1, D), jnp.float32).at[rows.reshape(-1)].add(contrib.reshape(-1, D))
    out = hid.reshape(rows_all, D) + total[:rows_all]
    return out.astype(jnp.bfloat16).reshape(MB, ROWS, D)

def reference(hidden, norm_gain, routes, route_weight, w_in, w_out):
    return expert_block(hidden, norm_gain, routes, route_weight, w_in, w_out)
```

```python
import jax
import jax.numpy as jnp
from jax import lax
from jax.sharding import PartitionSpec as P

EPS = 1e-06
LANES = 128


def route_tables(routes_now, weight_now, n_dev, cap, span):
    rows, top = routes_now.shape
    flat = routes_now.reshape(-1)
    order = jnp.arange(flat.shape[0], dtype=jnp.int32)
    earlier = (flat[None, :] == flat[:, None]) & (order[None, :] < order[:, None])
    rank = jnp.sum(earlier.astype(jnp.int32), axis=1)
    target = jnp.arange(n_dev * cap, dtype=jnp.int32)
    target_group = target // (cap * span)
    target_place = target % cap
    landing = (flat[None, :] == target_group[:, None]) & (rank[None, :] == target_place[:, None])
    landing = landing.reshape(n_dev * cap, rows, top)
    select = jnp.any(landing, axis=2).astype(jnp.bfloat16)
    weigh = jnp.sum(jnp.where(landing, weight_now[None, :, :], jnp.float32(0.0)), axis=2)
    return (select, weigh)


def packed_blocks(hidden, norm_gain, routes, route_weight, w_in, w_out):
    batches, rows, width = hidden.shape
    n_dev = lax.axis_size("dev")
    n_sub = lax.axis_size("sub")
    experts = n_dev // 2
    top = routes.shape[2]
    cap = max(2, 2 * rows * top // experts)
    span = n_dev // experts
    hid = hidden.astype(jnp.float32)
    normed = (
        hid * lax.rsqrt(jnp.mean(hid * hid, axis=-1, keepdims=True) + EPS) * norm_gain
    ).astype(jnp.bfloat16)
    part_width = width // n_sub
    offset = lax.axis_index("sub") * part_width
    tables = [
        route_tables(routes[step], route_weight[step], n_dev, cap, span) for step in range(batches)
    ]
    buffers = [
        jnp.dot(tables[step][0], normed[step], preferred_element_type=jnp.float32)
        .astype(jnp.bfloat16)
        .reshape(n_dev, cap, -1)
        for step in range(batches)
    ]

    def run_expert(arrived):
        senders, count, features = arrived.shape
        inner = jnp.dot(
            arrived.reshape(senders * count, features), w_in, preferred_element_type=jnp.float32
        )
        act = jax.nn.silu(inner).astype(jnp.bfloat16)
        pieces = jnp.dot(act, w_out, preferred_element_type=jnp.float32).astype(jnp.bfloat16)
        return lax.all_to_all(
            pieces.reshape(senders, count, -1), "dev", split_axis=0, concat_axis=0, tiled=True
        )

    def dispatch(buffer):
        returned = run_expert(
            lax.all_to_all(buffer, "dev", split_axis=0, concat_axis=0, tiled=True)
        )
        return returned

    returned = [dispatch(buffer) for buffer in buffers]
    terms = []
    for step in range(batches):
        flat_back = returned[step].reshape(n_dev * cap, width).astype(jnp.float32)
        terms.append(
            jnp.dot(
                tables[step][1].T,
                flat_back,
                precision=lax.Precision.HIGHEST,
                preferred_element_type=jnp.float32,
            )
        )
    summed = lax.psum_scatter(
        jnp.stack(terms).astype(jnp.bfloat16), "sub", scatter_dimension=2, tiled=True
    ).astype(jnp.float32)
    own = lax.dynamic_slice_in_dim(hid, offset, part_width, 2)
    layer_out = (own + summed).astype(jnp.bfloat16)
    return layer_out


def swap_cores(value):
    return lax.ppermute(value, "sub", [(0, 1), (1, 0)])


def along(value, step, experts):
    pairs = [(2 * z + x, 2 * ((z + step) % experts) + x) for z in range(experts) for x in range(2)]
    return lax.ppermute(value, "dev", pairs)


def across(value, n_dev):
    return lax.ppermute(value, "dev", [(i, i ^ 1) for i in range(n_dev)])


def whole_blocks(hidden, norm_gain, routes, route_weight, w_in, w_out):
    batches, rows, width = hidden.shape
    n_dev = lax.axis_size("dev")
    experts = n_dev // 2
    core = lax.axis_index("sub")
    mine = lax.axis_index("dev") // 2
    w_in_other = swap_cores(w_in)
    w_out_other = swap_cores(w_out)

    hid = lax.dynamic_index_in_dim(hidden, core, 0, keepdims=False).astype(jnp.float32)
    route = lax.dynamic_index_in_dim(routes, core, 0, keepdims=False)
    weight = lax.dynamic_index_in_dim(route_weight, core, 0, keepdims=False)
    normed = (
        hid * lax.rsqrt(jnp.mean(hid * hid, axis=-1, keepdims=True) + EPS) * norm_gain
    ).astype(jnp.bfloat16)
    lane = jnp.arange(LANES, dtype=jnp.int32)[None, :]
    gate = sum(
        jnp.where(route[:, k : k + 1] == lane % experts, weight[:, k : k + 1], jnp.float32(0.0))
        for k in range(route.shape[1])
    )
    high = gate.astype(jnp.bfloat16).astype(jnp.float32)
    tail = jnp.where(lane < experts, high, jnp.where(lane < 2 * experts, gate - high, 0.0))
    block = jnp.concatenate([normed, tail.astype(jnp.bfloat16)], axis=1)

    order = [1, 3, 2]
    column = {0: block}
    for k in order:
        column[k] = along(block, k, experts)
    beside = {k: across(column[k], n_dev) for k in [0] + order}

    def expert(ks):
        x = jnp.concatenate([part[k] for k in ks for part in (column, beside)], axis=0)
        gates = x[:, width:].astype(jnp.float32)
        keep = (lane == mine) | (lane == mine + experts)
        scale = jnp.sum(jnp.where(keep, gates, 0.0), axis=1, keepdims=True)
        x = x[:, :width]
        out = 0.0
        for up, down in ((w_in, w_out), (w_in_other, w_out_other)):
            inner = jnp.dot(x, up, preferred_element_type=jnp.float32)
            act = jax.nn.silu(inner).astype(jnp.bfloat16)
            out = out + jnp.dot(act, down, preferred_element_type=jnp.float32)
        out = (out * scale).astype(jnp.bfloat16).reshape(len(ks), 2, rows, width)
        return {k: out[i, 0] for i, k in enumerate(ks)}, {k: out[i, 1] for i, k in enumerate(ks)}

    own, give = {}, {}
    for ks in ([0, 1], [3], [2]):
        a, b = expert(ks)
        own.update(a)
        give.update(b)
    total = {}
    for k in [1, 3, 2, 0]:
        total[k] = own[k].astype(jnp.float32) + across(give[k], n_dev).astype(jnp.float32)
    result = hid + total[0]
    for k in order:
        result = result + along(total[k].astype(jnp.bfloat16), -k, experts).astype(jnp.float32)
    result = result.astype(jnp.bfloat16)
    half = width // 2
    kept = lax.dynamic_slice_in_dim(result, core * half, half, 1)
    passed = swap_cores(lax.dynamic_slice_in_dim(result, (1 - core) * half, half, 1))
    first = core == 0
    return jnp.stack([jnp.where(first, kept, passed), jnp.where(first, passed, kept)])


def local(hidden, norm_gain, routes, route_weight, w_in, w_out):
    batches, rows, _ = hidden.shape
    n_dev = lax.axis_size("dev")
    cap = max(2, 2 * rows * routes.shape[2] // (n_dev // 2))
    if cap >= rows and batches == lax.axis_size("sub") == 2 and n_dev == 8:
        return whole_blocks(hidden, norm_gain, routes, route_weight, w_in, w_out)
    return packed_blocks(hidden, norm_gain, routes, route_weight, w_in, w_out)


def solution(mesh):
    placed = (
        P(None, ("groups", "dev"), None),
        P(),
        P(None, ("groups", "dev"), None),
        P(None, ("groups", "dev"), None),
        P(None, ("dev", "sub")),
        P(("dev", "sub"), None),
    )
    return jax.shard_map(
        local,
        mesh=mesh,
        in_specs=placed,
        out_specs=P(None, ("groups", "dev"), "sub"),
        check_vma=False,
    )
```

```python
import functools

import jax
import jax.numpy as jnp
from jax import lax
from jax.experimental import pallas as pl
from jax.experimental.pallas import tpu as pltpu
from jax.sharding import PartitionSpec as P

EPS = 1e-06
LANES = 128
VMEM_BYTES = 24 << 20
LITTLE = pl.CostEstimate(flops=1, bytes_accessed=1, transcendentals=0)


def route_tables(routes_now, weight_now, n_dev, cap, span):
    rows, top = routes_now.shape
    flat = routes_now.reshape(-1)
    order = jnp.arange(flat.shape[0], dtype=jnp.int32)
    earlier = (flat[None, :] == flat[:, None]) & (order[None, :] < order[:, None])
    rank = jnp.sum(earlier.astype(jnp.int32), axis=1)
    target = jnp.arange(n_dev * cap, dtype=jnp.int32)
    target_group = target // (cap * span)
    target_place = target % cap
    landing = (flat[None, :] == target_group[:, None]) & (rank[None, :] == target_place[:, None])
    landing = landing.reshape(n_dev * cap, rows, top)
    select = jnp.any(landing, axis=2).astype(jnp.bfloat16)
    weigh = jnp.sum(jnp.where(landing, weight_now[None, :, :], jnp.float32(0.0)), axis=2)
    return (select, weigh)


def packed_blocks(hidden, norm_gain, routes, route_weight, w_in, w_out):
    batches, rows, width = hidden.shape
    n_dev = lax.axis_size("dev")
    n_sub = lax.axis_size("sub")
    experts = n_dev // 2
    top = routes.shape[2]
    cap = max(2, 2 * rows * top // experts)
    span = n_dev // experts
    hid = hidden.astype(jnp.float32)
    normed = (
        hid * lax.rsqrt(jnp.mean(hid * hid, axis=-1, keepdims=True) + EPS) * norm_gain
    ).astype(jnp.bfloat16)
    part_width = width // n_sub
    offset = lax.axis_index("sub") * part_width
    tables = [
        route_tables(routes[step], route_weight[step], n_dev, cap, span) for step in range(batches)
    ]
    buffers = [
        jnp.dot(tables[step][0], normed[step], preferred_element_type=jnp.float32)
        .astype(jnp.bfloat16)
        .reshape(n_dev, cap, -1)
        for step in range(batches)
    ]

    def run_expert(arrived):
        senders, count, features = arrived.shape
        inner = jnp.dot(
            arrived.reshape(senders * count, features), w_in, preferred_element_type=jnp.float32
        )
        act = jax.nn.silu(inner).astype(jnp.bfloat16)
        pieces = jnp.dot(act, w_out, preferred_element_type=jnp.float32).astype(jnp.bfloat16)
        return lax.all_to_all(
            pieces.reshape(senders, count, -1), "dev", split_axis=0, concat_axis=0, tiled=True
        )

    def dispatch(buffer):
        returned = run_expert(
            lax.all_to_all(buffer, "dev", split_axis=0, concat_axis=0, tiled=True)
        )
        return returned

    returned = [dispatch(buffer) for buffer in buffers]
    terms = []
    for step in range(batches):
        flat_back = returned[step].reshape(n_dev * cap, width).astype(jnp.float32)
        terms.append(
            jnp.dot(
                tables[step][1].T,
                flat_back,
                precision=lax.Precision.HIGHEST,
                preferred_element_type=jnp.float32,
            )
        )
    summed = lax.psum_scatter(
        jnp.stack(terms).astype(jnp.bfloat16), "sub", scatter_dimension=2, tiled=True
    ).astype(jnp.float32)
    own = lax.dynamic_slice_in_dim(hid, offset, part_width, 2)
    layer_out = (own + summed).astype(jnp.bfloat16)
    return layer_out


def swap_cores(value):
    return lax.ppermute(value, "sub", [(0, 1), (1, 0)])


def along(value, step, experts):
    pairs = [(2 * z + x, 2 * (z ^ step) + x) for z in range(experts) for x in range(2)]
    return lax.ppermute(value, "dev", pairs)


def across(value, n_dev):
    return lax.ppermute(value, "dev", [(i, i ^ 1) for i in range(n_dev)])


def in_vmem(value):
    return pltpu.with_memory_space_constraint(value, pltpu.VMEM)


def in_hbm(value):
    return pltpu.with_memory_space_constraint(value, pltpu.HBM)


def pack_kernel(experts, core_ref, hidden_ref, gain_ref, routes_ref, weight_ref, block_ref):
    rows, width = hidden_ref.shape[1:]
    gain = gain_ref[...].reshape(1, width)
    hid = hidden_ref[0].astype(jnp.float32)
    mean = jnp.sum(hid * hid, axis=1, keepdims=True) * (1.0 / width)
    block_ref[:, :width] = (hid * lax.rsqrt(mean + EPS) * gain).astype(jnp.bfloat16)
    lane = lax.broadcasted_iota(jnp.int32, (rows, LANES), 1)
    gate = jnp.zeros((rows, LANES), jnp.float32)
    for k in range(routes_ref.shape[1]):
        named = routes_ref[0, k].reshape(rows, 1) == lane % experts
        gate = gate + jnp.where(named, weight_ref[0, k].reshape(rows, 1), 0.0)
    high = gate.astype(jnp.bfloat16).astype(jnp.float32)
    tail = jnp.where(lane < experts, high, jnp.where(lane < 2 * experts, gate - high, 0.0))
    block_ref[:, width:] = tail.astype(jnp.bfloat16)


def pack(core, hidden, norm_gain, routes, route_weight, experts):
    _, rows, width = hidden.shape
    top = routes.shape[2]
    own = lambda i, core: (core[0], 0, 0)
    return pl.pallas_call(
        functools.partial(pack_kernel, experts),
        grid_spec=pltpu.PrefetchScalarGridSpec(
            num_scalar_prefetch=1,
            grid=(1,),
            in_specs=[
                pl.BlockSpec((1, rows, width), own),
                pl.BlockSpec((width,), lambda i, core: (0,)),
                pl.BlockSpec((1, top, rows), own),
                pl.BlockSpec((1, top, rows), own),
            ],
            out_specs=pl.BlockSpec((rows, width + LANES), lambda i, core: (0, 0)),
        ),
        out_shape=pltpu.VMEM((rows, width + LANES), jnp.bfloat16),
        compiler_params=pltpu.CompilerParams(vmem_limit_bytes=VMEM_BYTES),
    )(
        core.reshape(1),
        in_hbm(hidden),
        in_hbm(norm_gain),
        in_hbm(routes.swapaxes(1, 2)),
        in_hbm(route_weight.swapaxes(1, 2)),
    )


def load_kernel(count, *refs):
    arrived = refs[-1]
    sources, places = refs[:count], refs[-count - 1 : -1]
    copies = [
        pltpu.make_async_copy(source, place, arrived.at[i])
        for i, (source, place) in enumerate(zip(sources, places))
    ]
    for copy in copies:
        copy.start()
    for copy in copies:
        copy.wait()


def load(arrays, after):
    count = len(arrays)
    return pl.pallas_call(
        functools.partial(load_kernel, count),
        in_specs=[pl.BlockSpec(memory_space=pltpu.HBM)] * count
        + [pl.BlockSpec(memory_space=pl.ANY)] * len(after),
        out_specs=[pl.BlockSpec(memory_space=pltpu.VMEM)] * count,
        out_shape=[pltpu.VMEM(a.shape, a.dtype) for a in arrays],
        scratch_shapes=[pltpu.SemaphoreType.DMA((count,))],
        compiler_params=pltpu.CompilerParams(vmem_limit_bytes=VMEM_BYTES),
    )(*[in_hbm(a) for a in arrays], *after)


def expert_kernel(count, experts, *refs):
    blocks, refs = refs[:count], refs[count:]
    in_refs, down_refs, out_refs = refs[:2], refs[2:4], refs[-count:]
    rows, width = out_refs[0].shape
    x = jnp.concatenate([block[...] for block in blocks], axis=0)
    lane = lax.broadcasted_iota(jnp.int32, x.shape[:1] + (LANES,), 1)
    mine = lax.axis_index("dev") // 2
    keep = (lane == mine) | (lane == mine + experts)
    scale = jnp.sum(
        jnp.where(keep, x[:, width:].astype(jnp.float32), 0.0), axis=1, keepdims=True
    )
    x = x[:, :width]
    acts = []
    for ref in in_refs:
        inner = jnp.dot(x, ref[...], preferred_element_type=jnp.float32)
        acts.append((inner / (1.0 + jnp.exp(-inner))).astype(jnp.bfloat16))
    step = width // 4
    for start in range(0, width, step):
        out = sum(
            jnp.dot(act, ref[:, start : start + step], preferred_element_type=jnp.float32)
            for act, ref in zip(acts, down_refs)
        )
        out = (out * scale).astype(jnp.bfloat16)
        for i, ref in enumerate(out_refs):
            ref[:, start : start + step] = out[i * rows : (i + 1) * rows]


def expert(blocks, weights, experts, after):
    count = len(blocks)
    rows, width = blocks[0].shape[0], weights[0].shape[0]
    hidden_units = 2 * weights[0].shape[1]
    whole = pl.BlockSpec(memory_space=pltpu.VMEM)
    return pl.pallas_call(
        functools.partial(expert_kernel, count, experts),
        in_specs=[whole] * (count + 4) + [pl.BlockSpec(memory_space=pl.ANY)] * len(after),
        out_specs=[whole] * count,
        out_shape=[pltpu.VMEM((rows, width), jnp.bfloat16)] * count,
        compiler_params=pltpu.CompilerParams(vmem_limit_bytes=VMEM_BYTES),
    )(*[in_vmem(v) for v in (*blocks, *weights)], *after)


def pass_after(value, after):
    place = pl.BlockSpec(memory_space=pl.ANY)
    return pl.pallas_call(
        lambda value_ref, after_ref, out_ref: None,
        in_specs=[place, place],
        out_specs=place,
        out_shape=jax.ShapeDtypeStruct(value.shape, value.dtype),
        input_output_aliases={0: 0},
        compiler_params=pltpu.CompilerParams(vmem_limit_bytes=VMEM_BYTES),
    )(in_vmem(value), in_vmem(after))


def whole_blocks(hidden, norm_gain, routes, route_weight, w_in, w_out):
    batches, rows, width = hidden.shape
    n_dev = lax.axis_size("dev")
    experts = n_dev // 2
    core = lax.axis_index("sub")
    others = [swap_cores(w_in), swap_cores(w_out)]
    block = pack(core, hidden, norm_gain, routes, route_weight, experts)

    column, beside = {0: block}, {}
    column[1] = along(block, 1, experts)
    beside[0] = across(block, n_dev)
    column[2] = along(block, 2, experts)
    w_in, w_out, w_out_other = load([w_in, w_out, others[1]], [in_vmem(others[0]), in_vmem(beside[0])])
    weights = [w_in, others[0], w_out, w_out_other]
    column[1] = pass_after(column[1], w_in)
    beside[1] = across(column[1], n_dev)
    column[3] = along(column[2], 1, experts)
    beside[2] = across(column[2], n_dev)
    beside[3] = across(column[3], n_dev)

    own, give = {}, {}
    own[0], give[0], own[1], give[1] = expert(
        [block, beside[0], column[1], beside[1]], weights, experts, []
    )
    back_own, back_give = along(own[1], 1, experts), along(give[1], 1, experts)
    own[2], give[2] = expert([column[2], beside[2]], weights, experts, [own[0]])
    own[3], give[3] = expert([column[3], beside[3]], weights, experts, [own[2], back_give])

    result = lax.dynamic_index_in_dim(hidden, core, 0, keepdims=False).astype(jnp.float32)
    result = result + own[0].astype(jnp.float32) + back_own.astype(jnp.float32)
    for k in (2, 3):
        total = own[k].astype(jnp.float32) + across(give[k], n_dev).astype(jnp.float32)
        result = result + along(total.astype(jnp.bfloat16), k, experts).astype(jnp.float32)
    passed_on = give[0].astype(jnp.float32) + back_give.astype(jnp.float32)
    passed_on = across(passed_on.astype(jnp.bfloat16), n_dev)
    result = (result + passed_on.astype(jnp.float32)).astype(jnp.bfloat16)

    half = width // 2
    kept = lax.dynamic_slice_in_dim(result, core * half, half, 1)
    passed = swap_cores(lax.dynamic_slice_in_dim(result, (1 - core) * half, half, 1))
    first = core == 0
    return jnp.stack([jnp.where(first, kept, passed), jnp.where(first, passed, kept)])


def local(hidden, norm_gain, routes, route_weight, w_in, w_out):
    batches, rows, _ = hidden.shape
    n_dev = lax.axis_size("dev")
    cap = max(2, 2 * rows * routes.shape[2] // (n_dev // 2))
    if cap >= rows and n_dev == 8 and batches == lax.axis_size("sub") == 2:
        return whole_blocks(hidden, norm_gain, routes, route_weight, w_in, w_out)
    return packed_blocks(hidden, norm_gain, routes, route_weight, w_in, w_out)


def solution(mesh):
    placed = (
        P(None, ("groups", "dev"), None),
        P(),
        P(None, ("groups", "dev"), None),
        P(None, ("groups", "dev"), None),
        P(None, ("dev", "sub")),
        P(("dev", "sub"), None),
    )
    return jax.shard_map(
        local,
        mesh=mesh,
        in_specs=placed,
        out_specs=P(None, ("groups", "dev"), "sub"),
        check_vma=False,
    )
```

```python
import functools

import jax
import jax.numpy as jnp
from jax import lax
from jax.experimental import pallas as pl
from jax.experimental.pallas import tpu as pltpu
from jax.sharding import PartitionSpec as P

EPS = 1e-06
LANES = 128
TOKEN = (8, LANES)
VMEM_BYTES = 16 << 20


def route_tables(routes_now, weight_now, n_dev, cap, span):
    rows, top = routes_now.shape
    flat = routes_now.reshape(-1)
    order = jnp.arange(flat.shape[0], dtype=jnp.int32)
    earlier = (flat[None, :] == flat[:, None]) & (order[None, :] < order[:, None])
    rank = jnp.sum(earlier.astype(jnp.int32), axis=1)
    target = jnp.arange(n_dev * cap, dtype=jnp.int32)
    target_group = target // (cap * span)
    target_place = target % cap
    landing = (flat[None, :] == target_group[:, None]) & (rank[None, :] == target_place[:, None])
    landing = landing.reshape(n_dev * cap, rows, top)
    select = jnp.any(landing, axis=2).astype(jnp.bfloat16)
    weigh = jnp.sum(jnp.where(landing, weight_now[None, :, :], jnp.float32(0.0)), axis=2)
    return (select, weigh)


def packed_blocks(hidden, norm_gain, routes, route_weight, w_in, w_out):
    batches, rows, width = hidden.shape
    n_dev = lax.axis_size("dev")
    n_sub = lax.axis_size("sub")
    experts = n_dev // 2
    top = routes.shape[2]
    cap = max(2, 2 * rows * top // experts)
    span = n_dev // experts
    hid = hidden.astype(jnp.float32)
    normed = (
        hid * lax.rsqrt(jnp.mean(hid * hid, axis=-1, keepdims=True) + EPS) * norm_gain
    ).astype(jnp.bfloat16)
    part_width = width // n_sub
    offset = lax.axis_index("sub") * part_width
    tables = [
        route_tables(routes[step], route_weight[step], n_dev, cap, span) for step in range(batches)
    ]
    buffers = [
        jnp.dot(tables[step][0], normed[step], preferred_element_type=jnp.float32)
        .astype(jnp.bfloat16)
        .reshape(n_dev, cap, -1)
        for step in range(batches)
    ]

    def run_expert(arrived):
        senders, count, features = arrived.shape
        inner = jnp.dot(
            arrived.reshape(senders * count, features), w_in, preferred_element_type=jnp.float32
        )
        act = jax.nn.silu(inner).astype(jnp.bfloat16)
        pieces = jnp.dot(act, w_out, preferred_element_type=jnp.float32).astype(jnp.bfloat16)
        return lax.all_to_all(
            pieces.reshape(senders, count, -1), "dev", split_axis=0, concat_axis=0, tiled=True
        )

    def dispatch(buffer):
        returned = run_expert(
            lax.all_to_all(buffer, "dev", split_axis=0, concat_axis=0, tiled=True)
        )
        return returned

    returned = [dispatch(buffer) for buffer in buffers]
    terms = []
    for step in range(batches):
        flat_back = returned[step].reshape(n_dev * cap, width).astype(jnp.float32)
        terms.append(
            jnp.dot(
                tables[step][1].T,
                flat_back,
                precision=lax.Precision.HIGHEST,
                preferred_element_type=jnp.float32,
            )
        )
    summed = lax.psum_scatter(
        jnp.stack(terms).astype(jnp.bfloat16), "sub", scatter_dimension=2, tiled=True
    ).astype(jnp.float32)
    own = lax.dynamic_slice_in_dim(hid, offset, part_width, 2)
    layer_out = (own + summed).astype(jnp.bfloat16)
    return layer_out


def in_vmem(value):
    return pltpu.with_memory_space_constraint(value, pltpu.VMEM)


def in_hbm(value):
    return pltpu.with_memory_space_constraint(value, pltpu.HBM)


def swap_cores(value):
    return lax.ppermute(value, "sub", [(0, 1), (1, 0)])


def along(value, step, experts):
    pairs = [(2 * z + x, 2 * (z ^ step) + x) for z in range(experts) for x in range(2)]
    return lax.ppermute(value, "dev", pairs)


def along_to_core(value, step, experts, other):
    pairs = [
        (4 * z + 2 * x + s, 4 * (z ^ step) + 2 * x + (s ^ other))
        for z in range(experts)
        for x in range(2)
        for s in range(2)
    ]
    return lax.ppermute(value, ("dev", "sub"), pairs)


def across(value, n_dev):
    return lax.ppermute(value, "dev", [(i, i ^ 1) for i in range(n_dev)])


def kernel_call(kernel, operands, outs, after=(), hbm=0, scratch=()):
    vmem = pl.BlockSpec(memory_space=pltpu.VMEM)
    kept = [pl.BlockSpec(memory_space=pltpu.HBM)] * hbm + [vmem] * (len(operands) - hbm)
    count = len(operands)

    def body(*refs):
        kernel(*refs[:count], *refs[count + len(after) : count + len(after) + len(outs)], *refs[count + len(after) + len(outs) + 1 :])
        refs[count + len(after) + len(outs)][...] = jnp.zeros(TOKEN, jnp.float32)

    *given, token = pl.pallas_call(
        body,
        in_specs=kept + [pl.BlockSpec(memory_space=pl.ANY)] * len(after),
        out_specs=[vmem] * (len(outs) + 1),
        out_shape=[pltpu.VMEM(shape, dtype) for shape, dtype in [*outs, (TOKEN, jnp.float32)]],
        scratch_shapes=scratch,
        compiler_params=pltpu.CompilerParams(vmem_limit_bytes=VMEM_BYTES),
    )(
        *[in_hbm(v) for v in operands[:hbm]],
        *[in_vmem(v) for v in operands[hbm:]],
        *[in_vmem(v) for v in after],
    )
    return given, token


def pack_kernel(experts, core_ref, hidden_ref, gain_ref, routes_ref, weight_ref, block_ref):
    rows, width = hidden_ref.shape[1:]
    gain = gain_ref[...].reshape(1, width)
    hid = hidden_ref[0].astype(jnp.float32)
    mean = jnp.sum(hid * hid, axis=1, keepdims=True) * (1.0 / width)
    block_ref[:, :width] = (hid * lax.rsqrt(mean + EPS) * gain).astype(jnp.bfloat16)
    lane = lax.broadcasted_iota(jnp.int32, (rows, LANES), 1)
    gate = jnp.zeros((rows, LANES), jnp.float32)
    for k in range(routes_ref.shape[1]):
        named = routes_ref[0, k].reshape(rows, 1) == lane % experts
        gate = gate + jnp.where(named, weight_ref[0, k].reshape(rows, 1), 0.0)
    high = gate.astype(jnp.bfloat16).astype(jnp.float32)
    tail = jnp.where(lane < experts, high, jnp.where(lane < 2 * experts, gate - high, 0.0))
    block_ref[:, width:] = tail.astype(jnp.bfloat16)


def pack(core, hidden, norm_gain, routes, route_weight, experts):
    _, rows, width = hidden.shape
    top = routes.shape[2]
    own = lambda i, core: (core[0], 0, 0)
    return pl.pallas_call(
        functools.partial(pack_kernel, experts),
        grid_spec=pltpu.PrefetchScalarGridSpec(
            num_scalar_prefetch=1,
            grid=(1,),
            in_specs=[
                pl.BlockSpec((1, rows, width), own),
                pl.BlockSpec((width,), lambda i, core: (0,)),
                pl.BlockSpec((1, top, rows), own),
                pl.BlockSpec((1, top, rows), own),
            ],
            out_specs=pl.BlockSpec((rows, width + LANES), lambda i, core: (0, 0)),
        ),
        out_shape=pltpu.VMEM((rows, width + LANES), jnp.bfloat16),
        compiler_params=pltpu.CompilerParams(vmem_limit_bytes=VMEM_BYTES),
    )(
        core.reshape(1),
        in_hbm(hidden),
        in_hbm(norm_gain),
        in_hbm(routes.swapaxes(1, 2)),
        in_hbm(route_weight.swapaxes(1, 2)),
    )


def load(arrays, after):
    count = len(arrays)

    def kernel(*refs):
        arrived = refs[-1]
        copies = [
            pltpu.make_async_copy(source, place, arrived.at[i])
            for i, (source, place) in enumerate(zip(refs[:count], refs[count:-1]))
        ]
        for copy in copies:
            copy.start()
        for copy in copies:
            copy.wait()

    outs = [(a.shape, a.dtype) for a in arrays]
    return kernel_call(kernel, arrays, outs, after, count, [pltpu.SemaphoreType.DMA((count,))])


def expert(blocks, weights, experts, after):
    count = len(blocks)
    rows, width = blocks[0].shape[0], weights[0].shape[0]

    def kernel(*refs):
        ups, downs, out_refs = refs[count : count + 2], refs[count + 2 : count + 4], refs[count + 4 :]
        x = jnp.concatenate([block[...] for block in refs[:count]], axis=0)
        lane = lax.broadcasted_iota(jnp.int32, (count * rows, LANES), 1)
        mine = lax.axis_index("dev") // 2
        keep = (lane == mine) | (lane == mine + experts)
        gates = x[:, width:].astype(jnp.float32)
        scale = jnp.sum(jnp.where(keep, gates, 0.0), axis=1, keepdims=True)
        x = x[:, :width]
        acts = []
        for ref in ups:
            inner = jnp.dot(x, ref[...], preferred_element_type=jnp.float32)
            acts.append((inner / (1.0 + jnp.exp(-inner))).astype(jnp.bfloat16))
        step = width // 4
        for start in range(0, width, step):
            out = sum(
                jnp.dot(act, ref[:, start : start + step], preferred_element_type=jnp.float32)
                for act, ref in zip(acts, downs)
            )
            out = (out * scale).astype(jnp.bfloat16)
            for i, ref in enumerate(out_refs):
                ref[:, start : start + step] = out[i * rows : (i + 1) * rows]

    return kernel_call(
        kernel, [*blocks, *weights], [((rows, width), jnp.bfloat16)] * count, after
    )


def add(terms, after=(), dtype=jnp.bfloat16):
    def kernel(*refs):
        total = refs[0][...].astype(jnp.float32)
        for ref in refs[1:-1]:
            total = total + ref[...].astype(jnp.float32)
        refs[-1][...] = total.astype(dtype)

    (total,), token = kernel_call(kernel, terms, [(terms[0].shape, dtype)], after)
    return total, token


def add_halves(terms, dtype, after=()):
    rows, width = terms[0].shape
    half = width // 2

    def kernel(*refs):
        core = lax.axis_index("sub")
        for which, out_ref in ((core, refs[-2]), (1 - core, refs[-1])):
            place = pl.ds(pl.multiple_of(which * half, LANES), half)
            total = refs[0][:, place].astype(jnp.float32)
            for ref in refs[1:-2]:
                total = total + ref[:, place].astype(jnp.float32)
            out_ref[...] = total.astype(dtype)

    return kernel_call(kernel, terms, [((rows, half), dtype)] * 2, after)


def finish(kept, passed):
    def kernel(*refs):
        core = lax.axis_index("sub")
        out_ref = refs[-1]
        for place, refs in ((core, refs[: len(kept)]), (1 - core, refs[len(kept) : -1])):
            total = refs[0][...].astype(jnp.float32)
            for ref in refs[1:]:
                total = total + ref[...].astype(jnp.float32)
            out_ref[place] = total.astype(jnp.bfloat16)

    terms = [*kept, *passed]
    vmem = pl.BlockSpec(memory_space=pltpu.VMEM)
    return pl.pallas_call(
        kernel,
        in_specs=[vmem] * len(terms),
        out_specs=vmem,
        out_shape=jax.ShapeDtypeStruct((2, *kept[0].shape), jnp.bfloat16),
        compiler_params=pltpu.CompilerParams(vmem_limit_bytes=VMEM_BYTES),
    )(*[in_vmem(v) for v in terms])


def pass_after(value, after):
    place = pl.BlockSpec(memory_space=pl.ANY)
    return pl.pallas_call(
        lambda *refs: None,
        in_specs=[place] * (1 + len(after)),
        out_specs=place,
        out_shape=jax.ShapeDtypeStruct(value.shape, value.dtype),
        input_output_aliases={0: 0},
        compiler_params=pltpu.CompilerParams(vmem_limit_bytes=VMEM_BYTES),
    )(in_vmem(value), *[in_vmem(v) for v in after])


def whole_blocks(hidden, norm_gain, routes, route_weight, w_in, w_out):
    n_dev = lax.axis_size("dev")
    experts = n_dev // 2
    core = lax.axis_index("sub")
    others = [swap_cores(w_in), swap_cores(w_out)]
    block = pack(core, hidden, norm_gain, routes, route_weight, experts)
    column, beside = {0: block}, {}
    beside[0] = across(block, n_dev)
    column[2] = along(block, 2, experts)
    column[1] = along(block, 1, experts)
    (w_in, w_out, w_out_other), loaded = load([w_in, w_out, others[1]], [others[0], beside[0]])
    weights = [w_in, others[0], w_out, w_out_other]
    column[2] = pass_after(column[2], [loaded, column[1]])
    column[3] = along(column[2], 1, experts)
    beside[2] = across(column[2], n_dev)
    beside[3] = across(column[3], n_dev)
    again, _ = add([beside[0]], [column[3]])
    beside[1] = along(again, 1, experts)

    own, give, there = {}, {}, {}
    (own[2], give[2]), token = expert([column[2], beside[2]], weights, experts, [column[3]])
    there[2] = across(give[2], n_dev)
    (own[0], give[0], own[1], give[1]), token = expert(
        [block, beside[0], column[1], beside[1]], weights, experts, [token]
    )
    back_own, back_give = along(own[1], 1, experts), along(give[1], 1, experts)
    (own[3], give[3]), token = expert([column[3], beside[3]], weights, experts, [token])
    there[3] = across(give[3], n_dev)
    total, token = add([own[2], there[2]], [token])
    from_2 = along(total, 2, experts)
    total, token = add([own[3], there[3]], [token])
    last = along(total, 3, experts)
    total, _ = add([give[0], back_give], [token])
    there[0] = across(total, n_dev)
    partial, _ = add([own[0], back_own, from_2, last], [], jnp.float32)
    rows, width = own[0].shape
    half = width // 2
    result = lax.dynamic_index_in_dim(hidden, core, 0, keepdims=False).astype(jnp.float32)
    for part in (partial, there[0]):
        result = result + part.astype(jnp.float32)
    result = result.astype(jnp.bfloat16)
    kept = lax.dynamic_slice_in_dim(result, core * half, half, 1)
    passed = swap_cores(lax.dynamic_slice_in_dim(result, (1 - core) * half, half, 1))
    first = core == 0
    return jnp.stack([jnp.where(first, kept, passed), jnp.where(first, passed, kept)])


def local(hidden, norm_gain, routes, route_weight, w_in, w_out):
    batches, rows, _ = hidden.shape
    n_dev = lax.axis_size("dev")
    cap = max(2, 2 * rows * routes.shape[2] // (n_dev // 2))
    if cap >= rows and n_dev == 8 and batches == lax.axis_size("sub") == 2:
        return whole_blocks(hidden, norm_gain, routes, route_weight, w_in, w_out)
    return packed_blocks(hidden, norm_gain, routes, route_weight, w_in, w_out)


def solution(mesh):
    placed = (
        P(None, ("groups", "dev"), None),
        P(),
        P(None, ("groups", "dev"), None),
        P(None, ("groups", "dev"), None),
        P(None, ("dev", "sub")),
        P(("dev", "sub"), None),
    )
    return jax.shard_map(
        local,
        mesh=mesh,
        in_specs=placed,
        out_specs=P(None, ("groups", "dev"), "sub"),
        check_vma=False,
    )
```

```python
import functools

import jax
import jax.numpy as jnp
from jax import lax
from jax.experimental import pallas as pl
from jax.experimental.pallas import tpu as pltpu
from jax.sharding import PartitionSpec as P

EPS = 1e-06
LANES = 128
TOKEN = (8, LANES)
VMEM_BYTES = 16 << 20


def route_tables(routes_now, weight_now, n_dev, cap, span):
    rows, top = routes_now.shape
    flat = routes_now.reshape(-1)
    order = jnp.arange(flat.shape[0], dtype=jnp.int32)
    earlier = (flat[None, :] == flat[:, None]) & (order[None, :] < order[:, None])
    rank = jnp.sum(earlier.astype(jnp.int32), axis=1)
    target = jnp.arange(n_dev * cap, dtype=jnp.int32)
    target_group = target // (cap * span)
    target_place = target % cap
    landing = (flat[None, :] == target_group[:, None]) & (rank[None, :] == target_place[:, None])
    landing = landing.reshape(n_dev * cap, rows, top)
    select = jnp.any(landing, axis=2).astype(jnp.bfloat16)
    weigh = jnp.sum(jnp.where(landing, weight_now[None, :, :], jnp.float32(0.0)), axis=2)
    return (select, weigh)


def packed_blocks(hidden, norm_gain, routes, route_weight, w_in, w_out):
    batches, rows, width = hidden.shape
    n_dev = lax.axis_size("dev")
    n_sub = lax.axis_size("sub")
    experts = n_dev // 2
    top = routes.shape[2]
    cap = max(2, 2 * rows * top // experts)
    span = n_dev // experts
    hid = hidden.astype(jnp.float32)
    normed = (
        hid * lax.rsqrt(jnp.mean(hid * hid, axis=-1, keepdims=True) + EPS) * norm_gain
    ).astype(jnp.bfloat16)
    part_width = width // n_sub
    offset = lax.axis_index("sub") * part_width
    tables = [
        route_tables(routes[step], route_weight[step], n_dev, cap, span) for step in range(batches)
    ]
    buffers = [
        jnp.dot(tables[step][0], normed[step], preferred_element_type=jnp.float32)
        .astype(jnp.bfloat16)
        .reshape(n_dev, cap, -1)
        for step in range(batches)
    ]

    def run_expert(arrived):
        senders, count, features = arrived.shape
        inner = jnp.dot(
            arrived.reshape(senders * count, features), w_in, preferred_element_type=jnp.float32
        )
        act = jax.nn.silu(inner).astype(jnp.bfloat16)
        pieces = jnp.dot(act, w_out, preferred_element_type=jnp.float32).astype(jnp.bfloat16)
        return lax.all_to_all(
            pieces.reshape(senders, count, -1), "dev", split_axis=0, concat_axis=0, tiled=True
        )

    def dispatch(buffer):
        returned = run_expert(
            lax.all_to_all(buffer, "dev", split_axis=0, concat_axis=0, tiled=True)
        )
        return returned

    returned = [dispatch(buffer) for buffer in buffers]
    terms = []
    for step in range(batches):
        flat_back = returned[step].reshape(n_dev * cap, width).astype(jnp.float32)
        terms.append(
            jnp.dot(
                tables[step][1].T,
                flat_back,
                precision=lax.Precision.HIGHEST,
                preferred_element_type=jnp.float32,
            )
        )
    summed = lax.psum_scatter(
        jnp.stack(terms).astype(jnp.bfloat16), "sub", scatter_dimension=2, tiled=True
    ).astype(jnp.float32)
    own = lax.dynamic_slice_in_dim(hid, offset, part_width, 2)
    layer_out = (own + summed).astype(jnp.bfloat16)
    return layer_out


def in_vmem(value):
    return pltpu.with_memory_space_constraint(value, pltpu.VMEM)


def in_hbm(value):
    return pltpu.with_memory_space_constraint(value, pltpu.HBM)


def swap_cores(value):
    return lax.ppermute(value, "sub", [(0, 1), (1, 0)])


def along(value, step, experts):
    pairs = [(2 * z + x, 2 * (z ^ step) + x) for z in range(experts) for x in range(2)]
    return lax.ppermute(value, "dev", pairs)


def across(value, n_dev):
    return lax.ppermute(value, "dev", [(i, i ^ 1) for i in range(n_dev)])


def kernel_call(kernel, operands, outs, after=(), hbm=0, scratch=()):
    vmem = pl.BlockSpec(memory_space=pltpu.VMEM)
    kept = [pl.BlockSpec(memory_space=pltpu.HBM)] * hbm + [vmem] * (len(operands) - hbm)
    count = len(operands)
    first = count + len(after)
    last = first + len(outs)

    def body(*refs):
        kernel(*refs[:count], *refs[first:last], *refs[last + 1 :])
        refs[last][...] = jnp.zeros(TOKEN, jnp.float32)

    *given, token = pl.pallas_call(
        body,
        in_specs=kept + [pl.BlockSpec(memory_space=pl.ANY)] * len(after),
        out_specs=[vmem] * (len(outs) + 1),
        out_shape=[pltpu.VMEM(shape, dtype) for shape, dtype in [*outs, (TOKEN, jnp.float32)]],
        scratch_shapes=scratch,
        compiler_params=pltpu.CompilerParams(vmem_limit_bytes=VMEM_BYTES),
    )(
        *[in_hbm(v) for v in operands[:hbm]],
        *[in_vmem(v) for v in operands[hbm:]],
        *[in_vmem(v) for v in after],
    )
    return given, token


def pack_kernel(experts, core_ref, hidden_ref, gain_ref, routes_ref, weight_ref, block_ref):
    rows, width = hidden_ref.shape[1:]
    gain = gain_ref[...].reshape(1, width)
    hid = hidden_ref[0].astype(jnp.float32)
    mean = jnp.sum(hid * hid, axis=1, keepdims=True) * (1.0 / width)
    block_ref[:, :width] = (hid * lax.rsqrt(mean + EPS) * gain).astype(jnp.bfloat16)
    lane = lax.broadcasted_iota(jnp.int32, (rows, LANES), 1)
    gate = jnp.zeros((rows, LANES), jnp.float32)
    for k in range(routes_ref.shape[1]):
        named = routes_ref[0, k].reshape(rows, 1) == lane % experts
        gate = gate + jnp.where(named, weight_ref[0, k].reshape(rows, 1), 0.0)
    high = gate.astype(jnp.bfloat16).astype(jnp.float32)
    tail = jnp.where(lane < experts, high, jnp.where(lane < 2 * experts, gate - high, 0.0))
    block_ref[:, width:] = tail.astype(jnp.bfloat16)


def pack(core, hidden, norm_gain, routes, route_weight, experts):
    _, rows, width = hidden.shape
    top = routes.shape[2]
    own = lambda i, core: (core[0], 0, 0)
    return pl.pallas_call(
        functools.partial(pack_kernel, experts),
        grid_spec=pltpu.PrefetchScalarGridSpec(
            num_scalar_prefetch=1,
            grid=(1,),
            in_specs=[
                pl.BlockSpec((1, rows, width), own),
                pl.BlockSpec((width,), lambda i, core: (0,)),
                pl.BlockSpec((1, top, rows), own),
                pl.BlockSpec((1, top, rows), own),
            ],
            out_specs=pl.BlockSpec((rows, width + LANES), lambda i, core: (0, 0)),
        ),
        out_shape=pltpu.VMEM((rows, width + LANES), jnp.bfloat16),
        compiler_params=pltpu.CompilerParams(vmem_limit_bytes=VMEM_BYTES),
    )(
        core.reshape(1),
        in_hbm(hidden),
        in_hbm(norm_gain),
        in_hbm(routes.swapaxes(1, 2)),
        in_hbm(route_weight.swapaxes(1, 2)),
    )


def load(arrays, after):
    count = len(arrays)

    def kernel(*refs):
        arrived = refs[-1]
        copies = [
            pltpu.make_async_copy(source, place, arrived.at[i])
            for i, (source, place) in enumerate(zip(refs[:count], refs[count:-1]))
        ]
        for copy in copies:
            copy.start()
        for copy in copies:
            copy.wait()

    outs = [(a.shape, a.dtype) for a in arrays]
    return kernel_call(kernel, arrays, outs, after, count, [pltpu.SemaphoreType.DMA((count,))])


def expert(blocks, weights, experts, after=()):
    count = len(blocks)
    rows, width = blocks[0].shape[0], weights[0].shape[0]

    def kernel(*refs):
        ups, downs, out_refs = refs[count : count + 2], refs[count + 2 : count + 4], refs[count + 4 :]
        x = jnp.concatenate([block[...] for block in refs[:count]], axis=0)
        lane = lax.broadcasted_iota(jnp.int32, (count * rows, LANES), 1)
        mine = lax.axis_index("dev") // 2
        keep = (lane == mine) | (lane == mine + experts)
        gates = x[:, width:].astype(jnp.float32)
        scale = jnp.sum(jnp.where(keep, gates, 0.0), axis=1, keepdims=True)
        x = x[:, :width]
        acts = []
        for ref in ups:
            inner = jnp.dot(x, ref[...], preferred_element_type=jnp.float32)
            acts.append((inner / (1.0 + jnp.exp(-inner))).astype(jnp.bfloat16))
        step = width // 4
        for start in range(0, width, step):
            out = sum(
                jnp.dot(act, ref[:, start : start + step], preferred_element_type=jnp.float32)
                for act, ref in zip(acts, downs)
            )
            out = (out * scale).astype(jnp.bfloat16)
            for i, ref in enumerate(out_refs):
                ref[:, start : start + step] = out[i * rows : (i + 1) * rows]

    outs = [((rows, width), jnp.bfloat16)] * count
    return kernel_call(kernel, [*blocks, *weights], outs, after)


def add(terms, after=(), dtype=jnp.bfloat16):
    def kernel(*refs):
        total = refs[0][...].astype(jnp.float32)
        for ref in refs[1:-1]:
            total = total + ref[...].astype(jnp.float32)
        refs[-1][...] = total.astype(dtype)

    (total,), token = kernel_call(kernel, terms, [(terms[0].shape, dtype)], after)
    return total, token


def place(value, other, out=None):
    shape = (2, *value.shape)
    given = [value] if out is None else [value, out]

    def kernel(value_ref, *refs):
        out_ref, arrived = refs[-2:]
        core = lax.axis_index("sub")
        copy = pltpu.make_async_copy(value_ref, out_ref.at[1 - core if other else core], arrived)
        copy.start()
        copy.wait()

    return pl.pallas_call(
        kernel,
        in_specs=[pl.BlockSpec(memory_space=pltpu.VMEM)]
        + [pl.BlockSpec(memory_space=pltpu.HBM)] * (len(given) - 1),
        out_specs=pl.BlockSpec(memory_space=pltpu.HBM),
        out_shape=jax.ShapeDtypeStruct(shape, value.dtype),
        scratch_shapes=[pltpu.SemaphoreType.DMA],
        input_output_aliases={} if out is None else {1: 0},
        compiler_params=pltpu.CompilerParams(vmem_limit_bytes=VMEM_BYTES),
    )(in_vmem(value), *given[1:])


def pass_after(value, after):
    place = pl.BlockSpec(memory_space=pl.ANY)
    return pl.pallas_call(
        lambda *refs: None,
        in_specs=[place] * (1 + len(after)),
        out_specs=place,
        out_shape=jax.ShapeDtypeStruct(value.shape, value.dtype),
        input_output_aliases={0: 0},
        compiler_params=pltpu.CompilerParams(vmem_limit_bytes=VMEM_BYTES),
    )(in_vmem(value), *[in_vmem(v) for v in after])


def whole_blocks(hidden, norm_gain, routes, route_weight, w_in, w_out):
    n_dev = lax.axis_size("dev")
    experts = n_dev // 2
    core = lax.axis_index("sub")
    others = [swap_cores(w_in), swap_cores(w_out)]
    block = pack(core, hidden, norm_gain, routes, route_weight, experts)
    column, beside, own, give, there = {0: block}, {}, {}, {}, {}
    beside[0] = across(block, n_dev)
    column[2] = along(block, 2, experts)
    column[1] = along(block, 1, experts)
    (w_in, w_out, w_out_other), loaded = load([w_in, w_out, others[1]], [others[0]])
    weights = [w_in, others[0], w_out, w_out_other]
    column[2] = pass_after(column[2], [loaded, column[1]])
    column[3] = along(column[2], 1, experts)
    beside[2] = across(column[2], n_dev)
    beside[3] = across(column[3], n_dev)
    again, _ = add([beside[0]], [column[3]])
    beside[1] = along(again, 1, experts)

    (own[2], give[2]), token = expert([column[2], beside[2]], weights, experts)
    there[2] = across(give[2], n_dev)
    (own[0], give[0], own[1], give[1]), token = expert(
        [block, beside[0], column[1], beside[1]], weights, experts, [token]
    )
    back_own, back_give = along(own[1], 1, experts), along(give[1], 1, experts)
    (own[3], give[3]), token = expert([column[3], beside[3]], weights, experts, [token])
    there[3] = across(give[3], n_dev)
    total, token = add([own[2], there[2]], [token])
    from_2 = along(total, 2, experts)
    total, token = add([own[3], there[3]], [token])
    from_3 = along(total, 3, experts)
    total, _ = add([give[0], back_give], [token])
    there[0] = across(total, n_dev)

    partial, _ = add([own[0], back_own, from_2], dtype=jnp.float32)
    partial, _ = add([partial, from_3], dtype=jnp.float32)
    half = hidden.shape[2] // 2
    result = lax.dynamic_index_in_dim(hidden, core, 0, keepdims=False).astype(jnp.float32)
    result = (result + partial + there[0].astype(jnp.float32)).astype(jnp.bfloat16)
    kept = lax.dynamic_slice_in_dim(result, core * half, half, 1)
    passed = swap_cores(lax.dynamic_slice_in_dim(result, (1 - core) * half, half, 1))
    return place(passed, True, place(kept, False))


def local(hidden, norm_gain, routes, route_weight, w_in, w_out):
    batches, rows, _ = hidden.shape
    n_dev = lax.axis_size("dev")
    cap = max(2, 2 * rows * routes.shape[2] // (n_dev // 2))
    if cap >= rows and n_dev == 8 and batches == lax.axis_size("sub") == 2:
        return whole_blocks(hidden, norm_gain, routes, route_weight, w_in, w_out)
    return packed_blocks(hidden, norm_gain, routes, route_weight, w_in, w_out)


def solution(mesh):
    placed = (
        P(None, ("groups", "dev"), None),
        P(),
        P(None, ("groups", "dev"), None),
        P(None, ("groups", "dev"), None),
        P(None, ("dev", "sub")),
        P(("dev", "sub"), None),
    )
    return jax.shard_map(
        local,
        mesh=mesh,
        in_specs=placed,
        out_specs=P(None, ("groups", "dev"), "sub"),
        check_vma=False,
    )
```

```python
import functools

import jax
import jax.numpy as jnp
from jax import lax
from jax.experimental import pallas as pl
from jax.experimental.pallas import tpu as pltpu
from jax.sharding import PartitionSpec as P

EPS = 1e-06
LANES = 128
TOKEN = (8, LANES)
VMEM_BYTES = 16 << 20


def route_tables(routes_now, weight_now, n_dev, cap, span):
    rows, top = routes_now.shape
    flat = routes_now.reshape(-1)
    order = jnp.arange(flat.shape[0], dtype=jnp.int32)
    earlier = (flat[None, :] == flat[:, None]) & (order[None, :] < order[:, None])
    rank = jnp.sum(earlier.astype(jnp.int32), axis=1)
    target = jnp.arange(n_dev * cap, dtype=jnp.int32)
    target_group = target // (cap * span)
    target_place = target % cap
    landing = (flat[None, :] == target_group[:, None]) & (rank[None, :] == target_place[:, None])
    landing = landing.reshape(n_dev * cap, rows, top)
    select = jnp.any(landing, axis=2).astype(jnp.bfloat16)
    weigh = jnp.sum(jnp.where(landing, weight_now[None, :, :], jnp.float32(0.0)), axis=2)
    return (select, weigh)


def packed_blocks(hidden, norm_gain, routes, route_weight, w_in, w_out):
    batches, rows, width = hidden.shape
    n_dev = lax.axis_size("dev")
    n_sub = lax.axis_size("sub")
    experts = n_dev // 2
    top = routes.shape[2]
    cap = max(2, 2 * rows * top // experts)
    span = n_dev // experts
    hid = hidden.astype(jnp.float32)
    normed = (
        hid * lax.rsqrt(jnp.mean(hid * hid, axis=-1, keepdims=True) + EPS) * norm_gain
    ).astype(jnp.bfloat16)
    part_width = width // n_sub
    offset = lax.axis_index("sub") * part_width
    tables = [
        route_tables(routes[step], route_weight[step], n_dev, cap, span) for step in range(batches)
    ]
    buffers = [
        jnp.dot(tables[step][0], normed[step], preferred_element_type=jnp.float32)
        .astype(jnp.bfloat16)
        .reshape(n_dev, cap, -1)
        for step in range(batches)
    ]

    def run_expert(arrived):
        senders, count, features = arrived.shape
        inner = jnp.dot(
            arrived.reshape(senders * count, features), w_in, preferred_element_type=jnp.float32
        )
        act = jax.nn.silu(inner).astype(jnp.bfloat16)
        pieces = jnp.dot(act, w_out, preferred_element_type=jnp.float32).astype(jnp.bfloat16)
        return lax.all_to_all(
            pieces.reshape(senders, count, -1), "dev", split_axis=0, concat_axis=0, tiled=True
        )

    def dispatch(buffer):
        returned = run_expert(
            lax.all_to_all(buffer, "dev", split_axis=0, concat_axis=0, tiled=True)
        )
        return returned

    returned = [dispatch(buffer) for buffer in buffers]
    terms = []
    for step in range(batches):
        flat_back = returned[step].reshape(n_dev * cap, width).astype(jnp.float32)
        terms.append(
            jnp.dot(
                tables[step][1].T,
                flat_back,
                precision=lax.Precision.HIGHEST,
                preferred_element_type=jnp.float32,
            )
        )
    summed = lax.psum_scatter(
        jnp.stack(terms).astype(jnp.bfloat16), "sub", scatter_dimension=2, tiled=True
    ).astype(jnp.float32)
    own = lax.dynamic_slice_in_dim(hid, offset, part_width, 2)
    layer_out = (own + summed).astype(jnp.bfloat16)
    return layer_out


def in_vmem(value):
    return pltpu.with_memory_space_constraint(value, pltpu.VMEM)


def in_hbm(value):
    return pltpu.with_memory_space_constraint(value, pltpu.HBM)


def swap_cores(value):
    return lax.ppermute(value, "sub", [(0, 1), (1, 0)])


def along(value, step, experts):
    pairs = [(2 * z + x, 2 * (z ^ step) + x) for z in range(experts) for x in range(2)]
    return lax.ppermute(value, "dev", pairs)


def across(value, n_dev):
    return lax.ppermute(value, "dev", [(i, i ^ 1) for i in range(n_dev)])


def kernel_call(kernel, operands, outs, after=(), hbm=0, scratch=(), end=True):
    vmem = pl.BlockSpec(memory_space=pltpu.VMEM)
    kept = [pl.BlockSpec(memory_space=pltpu.HBM)] * hbm + [vmem] * (len(operands) - hbm)
    count = len(operands)
    first = count + len(after)
    last = first + len(outs)

    def body(*refs):
        kernel(*refs[:count], *refs[first:last], *refs[last + end :])
        if end:
            refs[last][...] = jnp.zeros(TOKEN, jnp.float32)

    tokens = [(TOKEN, jnp.float32)] * end
    given = pl.pallas_call(
        body,
        in_specs=kept + [pl.BlockSpec(memory_space=pl.ANY)] * len(after),
        out_specs=[vmem] * (len(outs) + end),
        out_shape=[pltpu.VMEM(shape, dtype) for shape, dtype in [*outs, *tokens]],
        scratch_shapes=scratch,
        compiler_params=pltpu.CompilerParams(vmem_limit_bytes=VMEM_BYTES),
    )(
        *[in_hbm(v) for v in operands[:hbm]],
        *[in_vmem(v) for v in operands[hbm:]],
        *[in_vmem(v) for v in after],
    )
    return given[: len(outs)], given[-1] if end else None


def pack_kernel(experts, core_ref, hidden_ref, gain_ref, routes_ref, weight_ref, block_ref):
    rows, width = hidden_ref.shape[1:]
    gain = gain_ref[...].reshape(1, width)
    hid = hidden_ref[0].astype(jnp.float32)
    mean = jnp.sum(hid * hid, axis=1, keepdims=True) * (1.0 / width)
    block_ref[:, :width] = (hid * lax.rsqrt(mean + EPS) * gain).astype(jnp.bfloat16)
    lane = lax.broadcasted_iota(jnp.int32, (rows, LANES), 1)
    gate = jnp.zeros((rows, LANES), jnp.float32)
    for k in range(routes_ref.shape[1]):
        named = routes_ref[0, k].reshape(rows, 1) == lane % experts
        gate = gate + jnp.where(named, weight_ref[0, k].reshape(rows, 1), 0.0)
    high = gate.astype(jnp.bfloat16).astype(jnp.float32)
    tail = jnp.where(lane < experts, high, jnp.where(lane < 2 * experts, gate - high, 0.0))
    block_ref[:, width:] = tail.astype(jnp.bfloat16)


def pack(core, hidden, norm_gain, routes, route_weight, experts):
    _, rows, width = hidden.shape
    top = routes.shape[2]
    own = lambda i, core: (core[0], 0, 0)
    return pl.pallas_call(
        functools.partial(pack_kernel, experts),
        grid_spec=pltpu.PrefetchScalarGridSpec(
            num_scalar_prefetch=1,
            grid=(1,),
            in_specs=[
                pl.BlockSpec((1, rows, width), own),
                pl.BlockSpec((width,), lambda i, core: (0,)),
                pl.BlockSpec((1, top, rows), own),
                pl.BlockSpec((1, top, rows), own),
            ],
            out_specs=pl.BlockSpec((rows, width + LANES), lambda i, core: (0, 0)),
        ),
        out_shape=pltpu.VMEM((rows, width + LANES), jnp.bfloat16),
        compiler_params=pltpu.CompilerParams(vmem_limit_bytes=VMEM_BYTES),
    )(
        core.reshape(1),
        in_hbm(hidden),
        in_hbm(norm_gain),
        in_hbm(routes.swapaxes(1, 2)),
        in_hbm(route_weight.swapaxes(1, 2)),
    )


def load(arrays, after):
    count = len(arrays)

    def kernel(*refs):
        arrived = refs[-1]
        copies = [
            pltpu.make_async_copy(source, place, arrived.at[i])
            for i, (source, place) in enumerate(zip(refs[:count], refs[count:-1]))
        ]
        for copy in copies:
            copy.start()
        for copy in copies:
            copy.wait()

    outs = [(a.shape, a.dtype) for a in arrays]
    return kernel_call(kernel, arrays, outs, after, count, [pltpu.SemaphoreType.DMA((count,))])


def expert(blocks, weights, experts, after=()):
    count = len(blocks)
    rows, width = blocks[0].shape[0], weights[0].shape[0]

    def kernel(*refs):
        ups, downs, out_refs = refs[count : count + 2], refs[count + 2 : count + 4], refs[count + 4 :]
        x = jnp.concatenate([block[...] for block in refs[:count]], axis=0)
        lane = lax.broadcasted_iota(jnp.int32, (count * rows, LANES), 1)
        mine = lax.axis_index("dev") // 2
        keep = (lane == mine) | (lane == mine + experts)
        gates = x[:, width:].astype(jnp.float32)
        scale = jnp.sum(jnp.where(keep, gates, 0.0), axis=1, keepdims=True)
        x = x[:, :width]
        acts = []
        for ref in ups:
            inner = jnp.dot(x, ref[...], preferred_element_type=jnp.float32)
            acts.append((inner / (1.0 + jnp.exp(-inner))).astype(jnp.bfloat16))
        step = width // 4
        for start in range(0, width, step):
            out = sum(
                jnp.dot(act, ref[:, start : start + step], preferred_element_type=jnp.float32)
                for act, ref in zip(acts, downs)
            )
            out = (out * scale).astype(jnp.bfloat16)
            for i, ref in enumerate(out_refs):
                ref[:, start : start + step] = out[i * rows : (i + 1) * rows]

    outs = [((rows, width), jnp.bfloat16)] * count
    return kernel_call(kernel, [*blocks, *weights], outs, after)


def add(terms, after=(), dtype=jnp.bfloat16, end=False):
    def kernel(*refs):
        total = refs[0][...].astype(jnp.float32)
        for ref in refs[1:-1]:
            total = total + ref[...].astype(jnp.float32)
        refs[-1][...] = total.astype(dtype)

    (total,), token = kernel_call(kernel, terms, [(terms[0].shape, dtype)], after, end=end)
    return total, token


def place(value, other, out=None):
    shape = (2, *value.shape)
    given = [value] if out is None else [value, out]

    def kernel(value_ref, *refs):
        out_ref, arrived = refs[-2:]
        core = lax.axis_index("sub")
        copy = pltpu.make_async_copy(value_ref, out_ref.at[1 - core if other else core], arrived)
        copy.start()
        copy.wait()

    return pl.pallas_call(
        kernel,
        in_specs=[pl.BlockSpec(memory_space=pltpu.VMEM)]
        + [pl.BlockSpec(memory_space=pltpu.HBM)] * (len(given) - 1),
        out_specs=pl.BlockSpec(memory_space=pltpu.HBM),
        out_shape=jax.ShapeDtypeStruct(shape, value.dtype),
        scratch_shapes=[pltpu.SemaphoreType.DMA],
        input_output_aliases={} if out is None else {1: 0},
        compiler_params=pltpu.CompilerParams(vmem_limit_bytes=VMEM_BYTES),
    )(in_vmem(value), *given[1:])


def pass_after(value, after):
    place = pl.BlockSpec(memory_space=pl.ANY)
    return pl.pallas_call(
        lambda *refs: None,
        in_specs=[place] * (1 + len(after)),
        out_specs=place,
        out_shape=jax.ShapeDtypeStruct(value.shape, value.dtype),
        input_output_aliases={0: 0},
        compiler_params=pltpu.CompilerParams(vmem_limit_bytes=VMEM_BYTES),
    )(in_vmem(value), *[in_vmem(v) for v in after])


def whole_blocks(hidden, norm_gain, routes, route_weight, w_in, w_out):
    n_dev = lax.axis_size("dev")
    experts = n_dev // 2
    core = lax.axis_index("sub")
    others = [swap_cores(w_in), swap_cores(w_out)]
    block = pack(core, hidden, norm_gain, routes, route_weight, experts)
    column, beside, own, give, there = {0: block}, {}, {}, {}, {}
    beside[0] = across(block, n_dev)
    column[2] = along(block, 2, experts)
    column[1] = along(block, 1, experts)
    (w_in, w_out, w_out_other), loaded = load([w_in, w_out, others[1]], [others[0]])
    weights = [w_in, others[0], w_out, w_out_other]
    column[2] = pass_after(column[2], [loaded, column[1]])
    column[3] = along(column[2], 1, experts)
    beside[2] = across(column[2], n_dev)
    beside[3] = across(column[3], n_dev)
    again, _ = add([beside[0]], [column[3]])
    beside[1] = along(again, 1, experts)

    (own[2], give[2]), token = expert([column[2], beside[2]], weights, experts)
    there[2] = across(give[2], n_dev)
    (own[0], give[0], own[1], give[1]), token = expert(
        [block, beside[0], column[1], beside[1]], weights, experts, [token]
    )
    back_own, back_give = along(own[1], 1, experts), along(give[1], 1, experts)
    (own[3], give[3]), token = expert([column[3], beside[3]], weights, experts, [token])
    there[3] = across(give[3], n_dev)
    total, token = add([own[2], there[2]], [token], end=True)
    from_2 = along(total, 2, experts)
    total, token = add([own[3], there[3]], [token], end=True)
    from_3 = along(total, 3, experts)
    total, _ = add([give[0], back_give], [token])
    there[0] = across(total, n_dev)

    partial, _ = add([own[0], back_own, from_2], dtype=jnp.float32)
    partial, _ = add([partial, from_3], dtype=jnp.float32)
    half = hidden.shape[2] // 2
    result = lax.dynamic_index_in_dim(hidden, core, 0, keepdims=False).astype(jnp.float32)
    result = (result + partial + there[0].astype(jnp.float32)).astype(jnp.bfloat16)
    kept = lax.dynamic_slice_in_dim(result, core * half, half, 1)
    passed = swap_cores(lax.dynamic_slice_in_dim(result, (1 - core) * half, half, 1))
    return place(passed, True, place(kept, False))


def local(hidden, norm_gain, routes, route_weight, w_in, w_out):
    batches, rows, _ = hidden.shape
    n_dev = lax.axis_size("dev")
    cap = max(2, 2 * rows * routes.shape[2] // (n_dev // 2))
    if cap >= rows and n_dev == 8 and batches == lax.axis_size("sub") == 2:
        return whole_blocks(hidden, norm_gain, routes, route_weight, w_in, w_out)
    return packed_blocks(hidden, norm_gain, routes, route_weight, w_in, w_out)


def solution(mesh):
    placed = (
        P(None, ("groups", "dev"), None),
        P(),
        P(None, ("groups", "dev"), None),
        P(None, ("groups", "dev"), None),
        P(None, ("dev", "sub")),
        P(("dev", "sub"), None),
    )
    return jax.shard_map(
        local,
        mesh=mesh,
        in_specs=placed,
        out_specs=P(None, ("groups", "dev"), "sub"),
        check_vma=False,
    )
```

```python
import functools

import jax
import jax.numpy as jnp
from jax import lax
from jax.experimental import pallas as pl
from jax.experimental.pallas import tpu as pltpu
from jax.sharding import PartitionSpec as P

EPS = 1e-06
LANES = 128
TOKEN = (8, LANES)
VMEM_BYTES = 16 << 20


def route_tables(routes_now, weight_now, n_dev, cap, span):
    rows, top = routes_now.shape
    flat = routes_now.reshape(-1)
    order = jnp.arange(flat.shape[0], dtype=jnp.int32)
    earlier = (flat[None, :] == flat[:, None]) & (order[None, :] < order[:, None])
    rank = jnp.sum(earlier.astype(jnp.int32), axis=1)
    target = jnp.arange(n_dev * cap, dtype=jnp.int32)
    target_group = target // (cap * span)
    target_place = target % cap
    landing = (flat[None, :] == target_group[:, None]) & (rank[None, :] == target_place[:, None])
    landing = landing.reshape(n_dev * cap, rows, top)
    select = jnp.any(landing, axis=2).astype(jnp.bfloat16)
    weigh = jnp.sum(jnp.where(landing, weight_now[None, :, :], jnp.float32(0.0)), axis=2)
    return (select, weigh)


def packed_blocks(hidden, norm_gain, routes, route_weight, w_in, w_out):
    batches, rows, width = hidden.shape
    n_dev = lax.axis_size("dev")
    n_sub = lax.axis_size("sub")
    experts = n_dev // 2
    top = routes.shape[2]
    cap = max(2, 2 * rows * top // experts)
    span = n_dev // experts
    hid = hidden.astype(jnp.float32)
    normed = (
        hid * lax.rsqrt(jnp.mean(hid * hid, axis=-1, keepdims=True) + EPS) * norm_gain
    ).astype(jnp.bfloat16)
    part_width = width // n_sub
    offset = lax.axis_index("sub") * part_width
    tables = [
        route_tables(routes[step], route_weight[step], n_dev, cap, span) for step in range(batches)
    ]
    buffers = [
        jnp.dot(tables[step][0], normed[step], preferred_element_type=jnp.float32)
        .astype(jnp.bfloat16)
        .reshape(n_dev, cap, -1)
        for step in range(batches)
    ]

    def run_expert(arrived):
        senders, count, features = arrived.shape
        inner = jnp.dot(
            arrived.reshape(senders * count, features), w_in, preferred_element_type=jnp.float32
        )
        act = jax.nn.silu(inner).astype(jnp.bfloat16)
        pieces = jnp.dot(act, w_out, preferred_element_type=jnp.float32).astype(jnp.bfloat16)
        return lax.all_to_all(
            pieces.reshape(senders, count, -1), "dev", split_axis=0, concat_axis=0, tiled=True
        )

    def dispatch(buffer):
        returned = run_expert(
            lax.all_to_all(buffer, "dev", split_axis=0, concat_axis=0, tiled=True)
        )
        return returned

    returned = [dispatch(buffer) for buffer in buffers]
    terms = []
    for step in range(batches):
        flat_back = returned[step].reshape(n_dev * cap, width).astype(jnp.float32)
        terms.append(
            jnp.dot(
                tables[step][1].T,
                flat_back,
                precision=lax.Precision.HIGHEST,
                preferred_element_type=jnp.float32,
            )
        )
    summed = lax.psum_scatter(
        jnp.stack(terms).astype(jnp.bfloat16), "sub", scatter_dimension=2, tiled=True
    ).astype(jnp.float32)
    own = lax.dynamic_slice_in_dim(hid, offset, part_width, 2)
    layer_out = (own + summed).astype(jnp.bfloat16)
    return layer_out


def in_vmem(value):
    return pltpu.with_memory_space_constraint(value, pltpu.VMEM)


def in_hbm(value):
    return pltpu.with_memory_space_constraint(value, pltpu.HBM)


def swap_cores(value):
    return lax.ppermute(value, "sub", [(0, 1), (1, 0)])


def along(value, step, experts):
    pairs = [(2 * z + x, 2 * (z ^ step) + x) for z in range(experts) for x in range(2)]
    return lax.ppermute(value, "dev", pairs)


def across(value, n_dev):
    return lax.ppermute(value, "dev", [(i, i ^ 1) for i in range(n_dev)])


def kernel_call(kernel, operands, outs, after=(), hbm=0, scratch=(), end=True):
    vmem = pl.BlockSpec(memory_space=pltpu.VMEM)
    kept = [pl.BlockSpec(memory_space=pltpu.HBM)] * hbm + [vmem] * (len(operands) - hbm)
    count = len(operands)
    first = count + len(after)
    last = first + len(outs)

    def body(*refs):
        kernel(*refs[:count], *refs[first:last], *refs[last + end :])
        if end:
            refs[last][...] = jnp.zeros(TOKEN, jnp.float32)

    tokens = [(TOKEN, jnp.float32)] * end
    given = pl.pallas_call(
        body,
        in_specs=kept + [pl.BlockSpec(memory_space=pl.ANY)] * len(after),
        out_specs=[vmem] * (len(outs) + end),
        out_shape=[pltpu.VMEM(shape, dtype) for shape, dtype in [*outs, *tokens]],
        scratch_shapes=scratch,
        compiler_params=pltpu.CompilerParams(vmem_limit_bytes=VMEM_BYTES),
    )(
        *[in_hbm(v) for v in operands[:hbm]],
        *[in_vmem(v) for v in operands[hbm:]],
        *[in_vmem(v) for v in after],
    )
    return given[: len(outs)], given[-1] if end else None


def pack_kernel(experts, core_ref, hidden_ref, gain_ref, routes_ref, weight_ref, block_ref):
    rows, width = hidden_ref.shape[1:]
    gain = gain_ref[...].reshape(1, width)
    hid = hidden_ref[0].astype(jnp.float32)
    mean = jnp.sum(hid * hid, axis=1, keepdims=True) * (1.0 / width)
    block_ref[:, :width] = (hid * lax.rsqrt(mean + EPS) * gain).astype(jnp.bfloat16)
    lane = lax.broadcasted_iota(jnp.int32, (rows, LANES), 1)
    gate = jnp.zeros((rows, LANES), jnp.float32)
    for k in range(routes_ref.shape[1]):
        named = routes_ref[0, k].reshape(rows, 1) == lane % experts
        gate = gate + jnp.where(named, weight_ref[0, k].reshape(rows, 1), 0.0)
    high = gate.astype(jnp.bfloat16).astype(jnp.float32)
    tail = jnp.where(lane < experts, high, jnp.where(lane < 2 * experts, gate - high, 0.0))
    block_ref[:, width:] = tail.astype(jnp.bfloat16)


def pack(core, hidden, norm_gain, routes, route_weight, experts):
    _, rows, width = hidden.shape
    top = routes.shape[2]
    own = lambda i, core: (core[0], 0, 0)
    return pl.pallas_call(
        functools.partial(pack_kernel, experts),
        grid_spec=pltpu.PrefetchScalarGridSpec(
            num_scalar_prefetch=1,
            grid=(1,),
            in_specs=[
                pl.BlockSpec((1, rows, width), own),
                pl.BlockSpec((width,), lambda i, core: (0,)),
                pl.BlockSpec((1, top, rows), own),
                pl.BlockSpec((1, top, rows), own),
            ],
            out_specs=pl.BlockSpec((rows, width + LANES), lambda i, core: (0, 0)),
        ),
        out_shape=pltpu.VMEM((rows, width + LANES), jnp.bfloat16),
        compiler_params=pltpu.CompilerParams(vmem_limit_bytes=VMEM_BYTES),
    )(
        core.reshape(1),
        in_hbm(hidden),
        in_hbm(norm_gain),
        in_hbm(routes.swapaxes(1, 2)),
        in_hbm(route_weight.swapaxes(1, 2)),
    )


def load(arrays, after):
    count = len(arrays)

    def kernel(*refs):
        arrived = refs[-1]
        copies = [
            pltpu.make_async_copy(source, place, arrived.at[i])
            for i, (source, place) in enumerate(zip(refs[:count], refs[count:-1]))
        ]
        for copy in copies:
            copy.start()
        for copy in copies:
            copy.wait()

    outs = [(a.shape, a.dtype) for a in arrays]
    return kernel_call(kernel, arrays, outs, after, count, [pltpu.SemaphoreType.DMA((count,))])


def expert(blocks, weights, experts, after=()):
    count = len(blocks)
    rows, width = blocks[0].shape[0], weights[0].shape[0]

    def kernel(*refs):
        ups, downs, out_refs = refs[count : count + 2], refs[count + 2 : count + 4], refs[count + 4 :]
        x = jnp.concatenate([block[...] for block in refs[:count]], axis=0)
        lane = lax.broadcasted_iota(jnp.int32, (count * rows, LANES), 1)
        mine = lax.axis_index("dev") // 2
        keep = (lane == mine) | (lane == mine + experts)
        gates = x[:, width:].astype(jnp.float32)
        scale = jnp.sum(jnp.where(keep, gates, 0.0), axis=1, keepdims=True)
        x = x[:, :width]
        acts = []
        for ref in ups:
            inner = jnp.dot(x, ref[...], preferred_element_type=jnp.float32)
            acts.append((inner / (1.0 + jnp.exp(-inner))).astype(jnp.bfloat16))
        step = width // 4
        for start in range(0, width, step):
            out = sum(
                jnp.dot(act, ref[:, start : start + step], preferred_element_type=jnp.float32)
                for act, ref in zip(acts, downs)
            )
            out = (out * scale).astype(jnp.bfloat16)
            for i, ref in enumerate(out_refs):
                ref[:, start : start + step] = out[i * rows : (i + 1) * rows]

    outs = [((rows, width), jnp.bfloat16)] * count
    return kernel_call(kernel, [*blocks, *weights], outs, after)


def add(terms, after=(), dtype=jnp.bfloat16, end=False):
    def kernel(*refs):
        total = refs[0][...].astype(jnp.float32)
        for ref in refs[1:-1]:
            total = total + ref[...].astype(jnp.float32)
        refs[-1][...] = total.astype(dtype)

    (total,), token = kernel_call(kernel, terms, [(terms[0].shape, dtype)], after, end=end)
    return total, token


def place(value, other, out=None):
    shape = (2, *value.shape)
    given = [value] if out is None else [value, out]

    def kernel(value_ref, *refs):
        out_ref, arrived = refs[-2:]
        core = lax.axis_index("sub")
        copy = pltpu.make_async_copy(value_ref, out_ref.at[1 - core if other else core], arrived)
        copy.start()
        copy.wait()

    return pl.pallas_call(
        kernel,
        in_specs=[pl.BlockSpec(memory_space=pltpu.VMEM)]
        + [pl.BlockSpec(memory_space=pltpu.HBM)] * (len(given) - 1),
        out_specs=pl.BlockSpec(memory_space=pltpu.HBM),
        out_shape=jax.ShapeDtypeStruct(shape, value.dtype),
        scratch_shapes=[pltpu.SemaphoreType.DMA],
        input_output_aliases={} if out is None else {1: 0},
        compiler_params=pltpu.CompilerParams(vmem_limit_bytes=VMEM_BYTES),
    )(in_vmem(value), *given[1:])


def pass_after(value, after):
    place = pl.BlockSpec(memory_space=pl.ANY)
    return pl.pallas_call(
        lambda *refs: None,
        in_specs=[place] * (1 + len(after)),
        out_specs=place,
        out_shape=jax.ShapeDtypeStruct(value.shape, value.dtype),
        input_output_aliases={0: 0},
        compiler_params=pltpu.CompilerParams(vmem_limit_bytes=VMEM_BYTES),
    )(in_vmem(value), *[in_vmem(v) for v in after])


def whole_blocks(hidden, norm_gain, routes, route_weight, w_in, w_out):
    n_dev = lax.axis_size("dev")
    experts = n_dev // 2
    core = lax.axis_index("sub")
    others = [swap_cores(w_in), swap_cores(w_out)]
    block = pack(core, hidden, norm_gain, routes, route_weight, experts)
    column, beside, own, give, there = {0: block}, {}, {}, {}, {}
    beside[0] = across(block, n_dev)
    column[2] = along(block, 2, experts)
    column[1] = along(block, 1, experts)
    (w_in, w_out, w_out_other), loaded = load([w_in, w_out, others[1]], [others[0]])
    weights = [w_in, others[0], w_out, w_out_other]
    column[2] = pass_after(column[2], [loaded, column[1]])
    column[3] = along(column[2], 1, experts)
    beside[2] = across(column[2], n_dev)
    beside[3] = across(column[3], n_dev)
    again, _ = add([beside[0]], [column[3]])
    beside[1] = along(again, 1, experts)

    (own[2], give[2]), token = expert([column[2], beside[2]], weights, experts)
    there[2] = across(give[2], n_dev)
    (own[0], give[0], own[1], give[1]), token = expert(
        [block, beside[0], column[1], beside[1]], weights, experts, [token]
    )
    back_own, back_give = along(own[1], 1, experts), along(give[1], 1, experts)
    (own[3], give[3]), token = expert([column[3], beside[3]], weights, experts, [token])
    there[3] = across(give[3], n_dev)
    total, token = add([own[2], there[2]], [token], end=True)
    from_2 = along(total, 2, experts)
    total, token = add([own[3], there[3]], [token], end=True)
    from_3 = along(total, 3, experts)
    total, _ = add([give[0], back_give], [token])
    there[0] = across(total, n_dev)

    partial, _ = add([own[0], back_own, from_2, from_3], dtype=jnp.float32)
    half = hidden.shape[2] // 2
    result = lax.dynamic_index_in_dim(hidden, core, 0, keepdims=False).astype(jnp.float32)
    result = (result + partial + there[0].astype(jnp.float32)).astype(jnp.bfloat16)
    kept = lax.dynamic_slice_in_dim(result, core * half, half, 1)
    passed = swap_cores(lax.dynamic_slice_in_dim(result, (1 - core) * half, half, 1))
    return place(passed, True, place(kept, False))


def local(hidden, norm_gain, routes, route_weight, w_in, w_out):
    batches, rows, _ = hidden.shape
    n_dev = lax.axis_size("dev")
    cap = max(2, 2 * rows * routes.shape[2] // (n_dev // 2))
    if cap >= rows and n_dev == 8 and batches == lax.axis_size("sub") == 2:
        return whole_blocks(hidden, norm_gain, routes, route_weight, w_in, w_out)
    return packed_blocks(hidden, norm_gain, routes, route_weight, w_in, w_out)


def solution(mesh):
    placed = (
        P(None, ("groups", "dev"), None),
        P(),
        P(None, ("groups", "dev"), None),
        P(None, ("groups", "dev"), None),
        P(None, ("dev", "sub")),
        P(("dev", "sub"), None),
    )
    return jax.shard_map(
        local,
        mesh=mesh,
        in_specs=placed,
        out_specs=P(None, ("groups", "dev"), "sub"),
        check_vma=False,
    )
```
